256 devices in a mesh: grp: 4 (over z_hi, core), vocab: 64 (over x, z_lo, y).
Axes of the slice: x: 4, y: 4, z: 8 (z_hi: 2, z_lo: 4; z = z_hi * 4 + z_lo), core: 2. Of those that a mesh axis runs over, the one named last changes fastest.
Arguments:
- teacher_hidden: bfloat16 [512, 8192], P('vocab', 'grp'), may hold values from -60 to 60
- norm_gain: float32 [8192], P('grp'), may hold values from 0.1 to 1.9
- teacher_weight: bfloat16 [8192, 81920], P('grp', 'vocab'), may hold values from -0.49718446 to 0.49718446
- student_hidden: bfloat16 [512, 3584], P('vocab', 'grp'), may hold values from -4 to 4
- student_weight: bfloat16 [3584, 81920], P('grp', 'vocab'), may hold values from -0.75167224 to 0.75167224
Outputs:
- kl_rows: float32 [512], P('grp')
- hidden_grad: float32 [512, 3584], P('vocab', 'grp')
The draws below stay inside these ranges and needn't reach their ends.
All inputs are finite; a program needn't handle non-finite values.
Results may differ from the reference program's by a relative error of at most 0.0071.
Values may be sent and summed in bfloat16 or wider, within the bound.
No kernel may reach another device: no remote copies, remote signals or barrier semaphores. Data moves between devices by JAX's collectives and lax.ppermute only.
A program may use at most 64 MiB of HBM per device.

```python
import math
import jax
import jax.numpy as jnp
from jax import lax

D_T = 8192
DS = 3584
TOKENS = 512
VOCAB = 81920


def column_scales(key, count, lowest, ratio):
    order_key = jax.random.fold_in(key, 77)
    pairs = count // 2
    order = jax.random.permutation(order_key, pairs)
    spot = order.astype(jnp.float32) / pairs
    scales = lowest * jnp.exp(spot * math.log(ratio))
    return jnp.repeat(scales, 2)


def head_matrix(key, depth, number, lowest, ratio):
    scales = column_scales(key, VOCAB, lowest, ratio)
    own_key = jax.random.fold_in(key, number)
    base = jnp.clip(jax.random.normal(own_key, (depth, VOCAB), jnp.float32), -6.0, 6.0)
    return base * scales[None, :] * depth ** (-0.5)


def draw_teacher_weight(key, part):
    matrix = head_matrix(key, D_T, 11, 0.4, 2.25)
    return matrix.astype(jnp.bfloat16)


def draw_student_weight(key, part):
    matrix = head_matrix(key, DS, 12, 0.4, 2.25)
    return matrix.astype(jnp.bfloat16)


def draw_teacher_hidden(key, part):
    own = jax.random.fold_in(key, 3)
    noise_key, row_key, col_key = jax.random.split(own, 3)
    row_scale = jnp.exp(jax.random.uniform(row_key, (TOKENS, 1), jnp.float32, 0.0, math.log(10.0)))
    spot = jnp.arange(D_T, dtype=jnp.float32) / D_T
    col_scale = jnp.exp(spot * math.log(3.0)) * jax.random.uniform(col_key, (D_T,), jnp.float32, 0.5, 1.5)
    noise = jnp.clip(jax.random.normal(noise_key, (TOKENS, D_T), jnp.float32), -6.0, 6.0)
    result = noise * row_scale * col_scale[None, :]
    return jnp.clip(result, -60.0, 60.0).astype(jnp.bfloat16)


def draw_student_hidden(key, part):
    own = jax.random.fold_in(key, 5)
    noise_key, col_key = jax.random.split(own, 2)
    col_scale = jax.random.uniform(col_key, (DS,), jnp.float32, 0.5, 1.5)
    result = jax.random.normal(noise_key, (TOKENS, DS), jnp.float32) * col_scale[None, :]
    return jnp.clip(result, -4.0, 4.0).astype(jnp.bfloat16)


def setup_inputs(seed: int = 0) -> dict:
    keys = jax.random.split(jax.random.key(seed), 6)
    return {
        "teacher_hidden": draw_teacher_hidden(jax.random.fold_in(keys[5], 71), 0),
        "norm_gain": jnp.clip(1.0 + 0.18 * jax.random.normal(keys[1], (D_T,), jnp.float32), 0.1, 1.9),
        "teacher_weight": draw_teacher_weight(jax.random.fold_in(keys[5], 71), 0),
        "student_hidden": draw_student_hidden(jax.random.fold_in(keys[5], 71), 0),
        "student_weight": draw_student_weight(jax.random.fold_in(keys[5], 71), 0),
    }


def reference(teacher_hidden, norm_gain, teacher_weight, student_hidden, student_weight):
    wide = teacher_hidden.astype(jnp.float32)
    mean_square = lax.optimization_barrier(jnp.mean(wide * wide, axis=1, keepdims=True))
    normed = (wide * lax.rsqrt(mean_square + 1e-06) * norm_gain[None, :]).astype(jnp.bfloat16)
    teacher_logits = jnp.dot(normed, teacher_weight, preferred_element_type=jnp.float32)
    student_logits = jnp.dot(student_hidden, student_weight, preferred_element_type=jnp.float32)
    teacher_log = jax.nn.log_softmax(teacher_logits, axis=1)
    student_log = jax.nn.log_softmax(student_logits, axis=1)
    teacher_prob = jnp.exp(teacher_log)
    kl_rows = lax.optimization_barrier(jnp.sum(teacher_prob * (teacher_log - student_log), axis=1))
    grad_logits = (jnp.exp(student_log) - teacher_prob).astype(jnp.bfloat16)
    hidden_grad = lax.dot_general(grad_logits, student_weight, (((1,), (1,)), ((), ())), preferred_element_type=jnp.float32)
    return (kl_rows, hidden_grad)
```

```python
import jax
import jax.numpy as jnp
from jax import lax
from jax.sharding import Mesh, PartitionSpec as P

D_T = 8192
EPS = 1e-06
GRP = ("zh", "c")
VOC = ("x", "zl", "y")
SIZE = {"zh": 2, "c": 2, "x": 4, "zl": 4, "y": 4}
GRAD_SCALE = 2.0**15


def shift(value, axis, distance):
    n = SIZE[axis]
    return lax.ppermute(value, axis, [(i, (i + distance) % n) for i in range(n)])


def gather4(value, axis):
    me = lax.axis_index(axis)
    rows = value.shape[0]
    blocks = [value] + [shift(value, axis, d) for d in (1, 2, 3)]
    out = jnp.zeros((4 * rows,) + value.shape[1:], value.dtype)
    for d in range(4):
        out = lax.dynamic_update_slice(out, blocks[d], (((me + 4 - d) % 4) * rows, 0))
    return out


def gather_hidden(value, cut):
    value = gather4(value, "zl")
    first, second = value[:, :cut], value[:, cut:]
    first, second = gather4(first, "y"), gather4(second, "x")
    first, second = gather4(first, "x"), gather4(second, "y")
    wide = second.shape[1]
    first = first.reshape(4, 4, 4, 8, cut)
    second = second.reshape(4, 4, 4, 8, wide).transpose(1, 2, 0, 3, 4)
    first = first.transpose(0, 2, 1, 3, 4)
    return jnp.concatenate([first.reshape(512, cut), second.reshape(512, wide)], axis=1)


def scatter_pair(value, axis):
    me = lax.axis_index(axis)
    give = lax.dynamic_index_in_dim(value, 1 - me, 0, keepdims=False).astype(jnp.float16)
    keep = lax.dynamic_index_in_dim(value, me, 0, keepdims=False)
    return keep + shift(give, axis, 1).astype(jnp.float32)


def logits_of(hidden, weight):
    terms = jnp.dot(hidden, weight, preferred_element_type=jnp.float32)
    terms = terms.reshape(2, 2, 128, 1280).transpose(1, 0, 2, 3)
    return scatter_pair(scatter_pair(terms, "c"), "zh")


def both(value, axis):
    me = lax.axis_index(axis)
    other = shift(value, axis, 1)
    return jnp.stack([jnp.where(me == 0, value, other), jnp.where(me == 0, other, value)])


def merge(stats, axis):
    parts = [stats] + [shift(stats, axis, d) for d in (1, 2, 3)]
    every = jnp.stack(parts)
    t_top = jnp.max(every[:, 0], axis=0)
    s_top = jnp.max(every[:, 3], axis=0)
    t_scale = jnp.exp(every[:, 0] - t_top)
    s_scale = jnp.exp(every[:, 3] - s_top)
    return jnp.stack(
        [
            t_top,
            jnp.sum(every[:, 1] * t_scale, axis=0),
            jnp.sum(every[:, 2] * t_scale, axis=0),
            s_top,
            jnp.sum(every[:, 4] * s_scale, axis=0),
        ]
    )


def scatter4(value, axis):
    me = lax.axis_index(axis)
    half = value.astype(jnp.float16)
    total = lax.dynamic_index_in_dim(value, me, 0, keepdims=False)
    for d in (1, 2, 3):
        give = lax.dynamic_index_in_dim(half, (me + d) % 4, 0, keepdims=False)
        total = total + shift(give, axis, d).astype(jnp.float32)
    return total


def scatter_grad(value):
    cut = 512
    first, second = value[:, :cut], value[:, cut:]
    wide = value.shape[1] - cut
    first = scatter4(first.reshape(4, 128, cut), "x")
    second = second.reshape(4, 4, 4, 8, wide).transpose(2, 0, 1, 3, 4)
    second = scatter4(second.reshape(4, 128, wide), "y")
    first = first.reshape(4, 4, 8, cut).transpose(1, 0, 2, 3).reshape(4, 32, cut)
    first = scatter4(first, "y")
    second = scatter4(second.reshape(4, 32, wide), "x")
    whole = jnp.concatenate([first, second], axis=1)
    return scatter4(whole.reshape(4, 8, value.shape[1]), "zl")


def on_device(teacher_hidden, norm_gain, teacher_weight, student_hidden, student_weight):
    student_rows = gather_hidden(student_hidden, 512)
    wide = teacher_hidden.astype(jnp.float32)
    squares = jnp.sum(wide * wide, axis=1)
    squares = squares + shift(squares, "c", 1)
    squares = squares + shift(squares, "zh", 1)
    inverse = lax.rsqrt(squares / D_T + EPS)
    normed = (wide * inverse[:, None] * norm_gain[None, :]).astype(jnp.bfloat16)
    student = logits_of(student_rows, student_weight)
    teacher = logits_of(gather_hidden(normed, 1024), teacher_weight)

    t_top = jnp.max(teacher, axis=1)
    s_top = jnp.max(student, axis=1)
    t_exp = jnp.exp(teacher - t_top[:, None])
    stats = jnp.stack(
        [
            t_top,
            jnp.sum(t_exp, axis=1),
            jnp.sum(t_exp * (teacher - student), axis=1),
            s_top,
            jnp.sum(jnp.exp(student - s_top[:, None]), axis=1),
        ]
    )
    for axis in ("y", "x", "zl"):
        stats = merge(stats, axis)
    t_log = stats[0] + jnp.log(stats[1])
    s_log = stats[3] + jnp.log(stats[4])
    kl_rows = stats[2] / stats[1] - t_log + s_log
    grad = jnp.exp(student - s_log[:, None]) - jnp.exp(teacher - t_log[:, None])
    grad = grad.astype(jnp.bfloat16)

    grad = both(grad, "zh")
    grad = both(grad.reshape(256, 1280), "c").reshape(2, 2, 128, 1280)
    grad = grad.transpose(1, 0, 2, 3).reshape(512, 1280)
    partial = lax.dot_general(
        grad, student_weight, (((1,), (1,)), ((), ())), preferred_element_type=jnp.float32
    )
    return kl_rows, scatter_grad(partial * GRAD_SCALE) * (1.0 / GRAD_SCALE)


def solution(mesh):
    fine = Mesh(mesh.devices.reshape(2, 2, 4, 4, 4), GRP + VOC)
    placed = (P(VOC, GRP), P(GRP), P(GRP, VOC), P(VOC, GRP), P(GRP, VOC))
    return jax.shard_map(
        on_device,
        mesh=fine,
        in_specs=placed,
        out_specs=(P(GRP), P(VOC, GRP)),
        check_vma=False,
    )
```

```python
import jax
import jax.numpy as jnp
from jax import lax
from jax.sharding import Mesh, PartitionSpec as P

D_T = 8192
EPS = 1e-06
GRP = ("zh", "c")
VOC = ("x", "zl", "y")
SIZE = {"zh": 2, "c": 2, "x": 4, "zl": 4, "y": 4}
GRAD_SCALE = 2.0**15


def shift(value, axis, distance):
    n = SIZE[axis]
    return lax.ppermute(value, axis, [(i, (i + distance) % n) for i in range(n)])


def gather4(value, axis, place):
    me = lax.axis_index(axis)
    came = {d: shift(value, axis, d) for d in (2, 1, 3)}
    blocks = [jnp.expand_dims(b, place) for b in (value, came[1], came[2], came[3])]
    shape = value.shape[:place] + (4,) + value.shape[place:]
    out = jnp.zeros(shape, value.dtype)
    for d in range(4):
        start = [0] * len(shape)
        start[place] = (me + 4 - d) % 4
        out = lax.dynamic_update_slice(out, blocks[d], start)
    return out


def gather_hidden(value, cut):
    value = gather4(value, "zl", 0)
    first, second = value[..., :cut], value[..., cut:]
    first = gather4(gather4(first, "y", 1), "x", 0)
    second = gather4(gather4(second, "x", 0), "y", 2)
    return first.reshape(512, -1), second.reshape(512, -1)


def scatter_pair(value, axis):
    me = lax.axis_index(axis)
    give = lax.dynamic_index_in_dim(value, 1 - me, 0, keepdims=False).astype(jnp.float16)
    keep = lax.dynamic_index_in_dim(value, me, 0, keepdims=False)
    return keep + shift(give, axis, 1).astype(jnp.float32)


def logits_of(hidden, weight):
    terms = jnp.dot(hidden, weight, preferred_element_type=jnp.float32)
    terms = terms.reshape(2, 2, 128, 1280).transpose(1, 0, 2, 3)
    return scatter_pair(scatter_pair(terms, "c"), "zh")


def pick(value, index, dim):
    return lax.dynamic_index_in_dim(value, index, dim, keepdims=False)


def grad_terms(mine, other, weight):
    def terms(grad):
        value = lax.dot_general(grad, weight, (((1,), (1,)), ((), ())), preferred_element_type=jnp.float32)
        return (value * GRAD_SCALE).astype(jnp.float16)

    return terms(mine), terms(other)


def in_order(mine, other, place):
    return jnp.where(place == 0, mine, other), jnp.where(place == 0, other, mine)


def scatter_grad(near, far):
    zh, c, zl = lax.axis_index("zh"), lax.axis_index("c"), lax.axis_index("zl")
    near, far = in_order(*near, c), in_order(*far, c)
    even, odd = in_order(near[0], far[0], zh), in_order(near[1], far[1], zh)
    terms = jnp.stack([even[0], odd[0], even[1], odd[1]])
    terms = terms.reshape(4, 4, 4, 8, 896).transpose(0, 2, 1, 3, 4)
    parts = lax.all_to_all(terms.reshape(16, 32, 896), ("x", "y"), 0, 0, tiled=True)
    total = jnp.sum(parts.astype(jnp.float32), axis=0).reshape(4, 8, 896)
    half = total.astype(jnp.float16)
    mine = pick(total, zl, 0)
    for d in (1, 2, 3):
        mine = mine + shift(pick(half, (zl + d) % 4, 0), "zl", d).astype(jnp.float32)
    return mine * (1.0 / GRAD_SCALE)


def merge(stats):
    padded = jnp.concatenate([stats, jnp.zeros((3, 128), jnp.float32)])
    every = lax.all_to_all(jnp.tile(padded, (64, 1)), VOC, 0, 0, tiled=True).reshape(64, 8, 128)
    t_top = jnp.max(every[:, 0], axis=0)
    s_top = jnp.max(every[:, 3], axis=0)
    t_scale = jnp.exp(every[:, 0] - t_top)
    s_scale = jnp.exp(every[:, 3] - s_top)
    t_total = jnp.sum(every[:, 1] * t_scale, axis=0)
    cross = jnp.sum(every[:, 2] * t_scale, axis=0)
    s_total = jnp.sum(every[:, 4] * s_scale, axis=0)
    return t_top + jnp.log(t_total), s_top + jnp.log(s_total), cross / t_total


def on_device(teacher_hidden, norm_gain, teacher_weight, student_hidden, student_weight):
    cut = 1536
    own = jnp.pad(teacher_hidden, ((0, 0), (0, 896))) + jnp.pad(student_hidden, ((0, 0), (2048, 0)))
    first, second = gather_hidden(own, cut)
    left = 2048 - cut
    wide = jnp.concatenate([first, second[:, :left]], axis=1).astype(jnp.float32)
    squares = jnp.sum(wide * wide, axis=1)
    squares = squares + shift(squares, "c", 1)
    squares = squares + shift(squares, "zh", 1)
    student = logits_of(second[:, left:], student_weight)
    inverse = lax.rsqrt(squares / D_T + EPS)
    normed = (wide * inverse[:, None] * norm_gain[None, :]).astype(jnp.bfloat16)
    teacher = logits_of(normed, teacher_weight)

    t_top = jnp.max(teacher, axis=1)
    s_top = jnp.max(student, axis=1)
    t_exp = jnp.exp(teacher - t_top[:, None])
    stats = jnp.stack(
        [
            t_top,
            jnp.sum(t_exp, axis=1),
            jnp.sum(t_exp * (teacher - student), axis=1),
            s_top,
            jnp.sum(jnp.exp(student - s_top[:, None]), axis=1),
        ]
    )
    t_log, s_log, cross = merge(stats)
    kl_rows = cross - t_log + s_log
    grad = jnp.exp(student - s_log[:, None]) - jnp.exp(teacher - t_log[:, None])
    grad = grad.astype(jnp.bfloat16)

    near = grad_terms(grad, shift(grad, "c", 1), student_weight)
    far, near = lax.optimization_barrier((shift(grad, "zh", 1), near))
    far = grad_terms(far, shift(far, "c", 1), student_weight)
    return kl_rows, scatter_grad(near, far)


def solution(mesh):
    fine = Mesh(mesh.devices.reshape(2, 2, 4, 4, 4), GRP + VOC)
    placed = (P(VOC, GRP), P(GRP), P(GRP, VOC), P(VOC, GRP), P(GRP, VOC))
    return jax.shard_map(
        on_device,
        mesh=fine,
        in_specs=placed,
        out_specs=(P(GRP), P(VOC, GRP)),
        check_vma=False,
    )
```

```python
import jax
import jax.numpy as jnp
from jax import lax
from jax.sharding import Mesh, PartitionSpec as P

D_T = 8192
EPS = 1e-06
GRP = ("zh", "c")
VOC = ("x", "zl", "y")
SIZE = {"zh": 2, "c": 2, "x": 4, "zl": 4, "y": 4}
GRAD_SCALE = 2.0**15


def shift(value, axis, distance):
    n = SIZE[axis]
    return lax.ppermute(value, axis, [(i, (i + distance) % n) for i in range(n)])


def gather4(value, axis, place, late=None):
    me = lax.axis_index(axis)
    came = {d: shift(value if d < 3 or late is None else late, axis, d) for d in (2, 1, 3)}
    blocks = [jnp.expand_dims(b, place) for b in (value, came[1], came[2], came[3])]
    shape = value.shape[:place] + (4,) + value.shape[place:]
    out = jnp.zeros(shape, value.dtype)
    for d in range(4):
        start = [0] * len(shape)
        start[place] = (me + 4 - d) % 4
        out = lax.dynamic_update_slice(out, blocks[d], start)
    return out


def gather_hidden(value, cut):
    value = gather4(value, "zl", 0)
    first, second = value[..., :cut], value[..., cut:]
    first = gather4(first, "y", 1)
    second = gather4(second, "x", 0)
    late, first = lax.optimization_barrier((second, first))
    first, second = gather4(first, "x", 0), gather4(second, "y", 2, late)
    return first.reshape(512, -1), second.reshape(512, -1)


def trade_pair(value, axis):
    me = lax.axis_index(axis)
    give = lax.dynamic_index_in_dim(value, 1 - me, 0, keepdims=False).astype(jnp.float16)
    return lax.dynamic_index_in_dim(value, me, 0, keepdims=False), shift(give, axis, 1)


def both_parts(kept, came):
    return kept + came.astype(jnp.float32)


def logits_of(hidden, weight):
    terms = jnp.dot(hidden, weight, preferred_element_type=jnp.float32)
    terms = terms.reshape(2, 2, 128, 1280).transpose(1, 0, 2, 3)
    return trade_pair(both_parts(*trade_pair(terms, "c")), "zh")


def pick(value, index, dim):
    return lax.dynamic_index_in_dim(value, index, dim, keepdims=False)


def grad_terms(mine, other, weight):
    def terms(grad):
        value = lax.dot_general(grad, weight, (((1,), (1,)), ((), ())), preferred_element_type=jnp.float32)
        return (value * GRAD_SCALE).astype(jnp.float16)

    return terms(mine), terms(other)


def in_order(mine, other, place):
    return jnp.where(place == 0, mine, other), jnp.where(place == 0, other, mine)


def scatter_grad(near, far):
    zh, c, zl = lax.axis_index("zh"), lax.axis_index("c"), lax.axis_index("zl")
    near, far = in_order(*near, c), in_order(*far, c)
    even, odd = in_order(near[0], far[0], zh), in_order(near[1], far[1], zh)
    terms = jnp.stack([even[0], odd[0], even[1], odd[1]])
    terms = terms.reshape(4, 4, 4, 8, 896).transpose(0, 2, 1, 3, 4)
    parts = lax.all_to_all(terms.reshape(16, 32, 896), ("x", "y"), 0, 0, tiled=True)
    total = jnp.sum(parts.astype(jnp.float32), axis=0).reshape(4, 8, 896)
    half = total.astype(jnp.float16)
    mine = pick(total, zl, 0)
    for d in (1, 2, 3):
        mine = mine + shift(pick(half, (zl + d) % 4, 0), "zl", d).astype(jnp.float32)
    return mine * (1.0 / GRAD_SCALE)


def merge(stats):
    padded = jnp.concatenate([stats, jnp.zeros((3, 128), jnp.float32)])
    every = lax.all_to_all(jnp.tile(padded, (64, 1)), VOC, 0, 0, tiled=True).reshape(64, 8, 128)
    t_top = jnp.max(every[:, 0], axis=0)
    s_top = jnp.max(every[:, 3], axis=0)
    t_scale = jnp.exp(every[:, 0] - t_top)
    s_scale = jnp.exp(every[:, 3] - s_top)
    t_total = jnp.sum(every[:, 1] * t_scale, axis=0)
    cross = jnp.sum(every[:, 2] * t_scale, axis=0)
    s_total = jnp.sum(every[:, 4] * s_scale, axis=0)
    return t_top + jnp.log(t_total), s_top + jnp.log(s_total), cross / t_total


def on_device(teacher_hidden, norm_gain, teacher_weight, student_hidden, student_weight):
    cut = 1536
    own = jnp.pad(teacher_hidden, ((0, 0), (0, 896))) + jnp.pad(student_hidden, ((0, 0), (2048, 0)))
    first, second = gather_hidden(own, cut)
    left = 2048 - cut
    wide = jnp.concatenate([first, second[:, :left]], axis=1).astype(jnp.float32)
    squares = jnp.sum(wide * wide, axis=1)
    squares = squares + shift(squares, "zh", 1)
    squares = squares + shift(squares, "c", 1)
    student = both_parts(*logits_of(second[:, left:], student_weight))
    inverse = lax.rsqrt(squares / D_T + EPS)
    normed = (wide * inverse[:, None] * norm_gain[None, :]).astype(jnp.bfloat16)
    kept, came = logits_of(normed, teacher_weight)

    s_top = jnp.max(student, axis=1)
    s_total = jnp.sum(jnp.exp(student - s_top[:, None]), axis=1)
    came, s_total = lax.optimization_barrier((came, s_total))
    teacher = both_parts(kept, came)
    t_top = jnp.max(teacher, axis=1)
    t_exp = jnp.exp(teacher - t_top[:, None])
    t_total, cross = jnp.sum(t_exp, axis=1), jnp.sum(t_exp * (teacher - student), axis=1)
    stats = jnp.stack([t_top, t_total, cross, s_top, s_total])
    t_log, s_log, cross = merge(stats)
    kl_rows = cross - t_log + s_log
    grad = jnp.exp(student - s_log[:, None]) - jnp.exp(teacher - t_log[:, None])
    grad = grad.astype(jnp.bfloat16)

    near = grad_terms(grad, shift(grad, "c", 1), student_weight)
    far, near = lax.optimization_barrier((shift(grad, "zh", 1), near))
    far = grad_terms(far, shift(far, "c", 1), student_weight)
    return kl_rows, scatter_grad(near, far)


def solution(mesh):
    fine = Mesh(mesh.devices.reshape(2, 2, 4, 4, 4), GRP + VOC)
    placed = (P(VOC, GRP), P(GRP), P(GRP, VOC), P(VOC, GRP), P(GRP, VOC))
    return jax.shard_map(
        on_device,
        mesh=fine,
        in_specs=placed,
        out_specs=(P(GRP), P(VOC, GRP)),
        check_vma=False,
    )
```
